512 devices in a mesh: row: 16 (over y, x_lo, core), col: 32 (over x_hi, z).
Axes of the slice: x: 4 (x_hi: 2, x_lo: 2; x = x_hi * 2 + x_lo), y: 4, z: 16, core: 2. Of those that a mesh axis runs over, the one named last changes fastest.
Arguments:
- vectors: bfloat16 [64, 196608], P(None, ('row', 'col')), may hold values from -6 to 6
- near_blocks: bfloat16 [16, 32, 6, 512, 512], P('row', 'col'), may hold values from -0.25 to 0.25
- far_left: bfloat16 [16, 32, 32, 12288], P('row', 'col'), may hold values from -1 to 1
- far_right: bfloat16 [16, 32, 32, 6144], P('row', 'col'), may hold values from -0.078125 to 0.078125
- far_mask: int32 [16, 32], P('row', 'col'), may hold values 0 or 1
- ranks: int32 [16, 32], P('row', 'col'), may hold values from 8 to 32
- near_rows: int32 [16, 32, 6], P('row', 'col'), may hold values from 0 to 23
- near_cols: int32 [16, 32, 6], P('row', 'col'), may hold values from 0 to 11
Outputs:
- product: float32 [64, 196608], P(None, ('row', 'col'))
The draws below stay inside these ranges and needn't reach their ends.
All inputs are finite; a program needn't handle non-finite values. No bound on the sum of `far_mask` on one device may be relied on, other than what follows from the above.
Results may differ from the reference program's by a relative error of at most 0.0024.
Values may be sent and summed in bfloat16 or wider, within the bound.
No kernel may reach another device: no remote copies, remote signals or barrier semaphores. Data moves between devices by JAX's collectives and lax.ppermute only.
A program may use at most 64 MiB of HBM per device.

```python
import jax
import jax.numpy as jnp
from jax import lax

W = 512
RANK = 32
SR = 24
NEAR = 6
NRHS = 64
GRID_R = 16
GRID_C = 32
S = 12288
C = 6144
SC = 12
ORDER = 196608


def place_ends(entries, own_key, smallest, high):
    extent = entries.shape
    index_at = [jax.random.randint(jax.random.fold_in(own_key, axis), (), 0, extent[axis]) for axis in range(len(extent))]
    entries = entries.at[tuple(index_at)].set(smallest)
    longest = extent.index(max(extent))
    index_at[longest] = (index_at[longest] + 1) % extent[longest]
    return entries.at[tuple(index_at)].set(high)


def block_scale(key, shape, pieces, least, top_value):
    factor_of = 1.0
    for position, parts in pieces:
        steps = jax.random.uniform(jax.random.fold_in(jax.random.fold_in(key, 6), position), (parts,), jnp.float32, least / len(pieces), top_value / len(pieces))
        factor_of = factor_of * jnp.repeat(jnp.exp(steps), shape[position] // parts).reshape((-1,) + (1,) * (len(shape) - 1 - position))
    return factor_of


def scatter_about(stream_key, shape, deviation, limit, shards=(), kind=jnp.bfloat16):
    result = jax.random.normal(stream_key, shape, jnp.float32) * deviation
    if len(shards) > 0:
        result = block_scale(stream_key, shape, shards, -0.22, 0.18) * result
    return jnp.clip(result, min=-limit, max=limit).astype(kind)


def setup_inputs(seed: int = 0) -> dict:
    streams_of = jax.random.split(jax.random.key(seed), 9)
    vectors = scatter_about(streams_of[0], (NRHS, ORDER), 1.0, 6.0, ((1, 512),))
    near_blocks = scatter_about(streams_of[1], (GRID_R, GRID_C, NEAR, W, W), W ** -0.5, 0.25, ((0, 16), (1, 32)))
    far_left = scatter_about(streams_of[2], (GRID_R, GRID_C, RANK, S), RANK ** -0.5, 1.0, ((0, 16), (1, 32)))
    far_right = scatter_about(streams_of[3], (GRID_R, GRID_C, RANK, C), C ** -0.5, 0.078125, ((0, 16), (1, 32)))
    far_mask = place_ends((jax.random.randint(streams_of[4], (GRID_R, GRID_C), 0, 2) < 1).astype(jnp.int32), jax.random.fold_in(streams_of[4], 1), 0, 1)
    ranks = place_ends(jax.random.randint(streams_of[5], (GRID_R, GRID_C), RANK // 4, RANK + 1), jax.random.fold_in(streams_of[5], 1), RANK // 4, RANK).astype(jnp.int32)
    near_rows = place_ends(jax.random.randint(streams_of[6], (GRID_R, GRID_C, NEAR), 0, SR), jax.random.fold_in(streams_of[6], 1), 0, SR - 1).astype(jnp.int32)
    near_cols = place_ends(jax.random.randint(streams_of[7], (GRID_R, GRID_C, NEAR), 0, SC), jax.random.fold_in(streams_of[7], 1), 0, SC - 1).astype(jnp.int32)
    return {"vectors": vectors, "near_blocks": near_blocks, "far_left": far_left, "far_right": far_right, "far_mask": far_mask, "ranks": ranks, "near_rows": near_rows, "near_cols": near_cols}


def tile_terms(row_vector, column_vector, blocks, left_factor, right_factor, far_flag, rank_value, rows_at, cols_at):
    vector_count = row_vector.shape[0]
    row_span = row_vector.shape[1]
    col_span = column_vector.shape[1]

    def far_branch():
        rank_keep = (jnp.arange(left_factor.shape[0], dtype=jnp.int32) < rank_value).astype(jnp.float32)
        coef_fwd = lax.dot_general(column_vector, right_factor, (((1,), (1,)), ((), ())), preferred_element_type=jnp.float32)
        coef_back = lax.dot_general(row_vector, left_factor, (((1,), (1,)), ((), ())), preferred_element_type=jnp.float32)
        coef_fwd = (coef_fwd * rank_keep).astype(jnp.bfloat16)
        coef_back = (coef_back * rank_keep).astype(jnp.bfloat16)
        forward = jnp.dot(coef_fwd, left_factor, preferred_element_type=jnp.float32)
        backward = jnp.dot(coef_back, right_factor, preferred_element_type=jnp.float32)
        return forward, backward

    def near_branch():
        block_width = blocks.shape[-1]
        forward = jnp.zeros((vector_count, row_span), jnp.float32)
        backward = jnp.zeros((vector_count, col_span), jnp.float32)
        for slot_index in range(blocks.shape[0]):
            row_start = (rows_at[slot_index] * block_width).astype(jnp.int32)
            col_start = (cols_at[slot_index] * block_width).astype(jnp.int32)
            piece_col = lax.dynamic_slice_in_dim(column_vector, col_start, block_width, 1)
            piece_row = lax.dynamic_slice_in_dim(row_vector, row_start, block_width, 1)
            add_fwd = lax.dot_general(piece_col, blocks[slot_index], (((1,), (1,)), ((), ())), preferred_element_type=jnp.float32)
            add_back = jnp.dot(piece_row, blocks[slot_index], preferred_element_type=jnp.float32)
            current_fwd = lax.dynamic_slice_in_dim(forward, row_start, block_width, 1)
            forward = lax.dynamic_update_slice_in_dim(forward, current_fwd + add_fwd, row_start, 1)
            current_back = lax.dynamic_slice_in_dim(backward, col_start, block_width, 1)
            backward = lax.dynamic_update_slice_in_dim(backward, current_back + add_back, col_start, 1)
        return forward, backward

    return lax.cond(far_flag > 0, far_branch, near_branch)


def reference(vectors, near_blocks, far_left, far_right, far_mask, ranks, near_rows, near_cols):
    def row_step(back_total, row_index):
        row_vector = lax.dynamic_slice_in_dim(vectors, (row_index * S).astype(jnp.int32), S, 1)

        def col_step(carry, col_index):
            fwd_total, back_inner = carry
            column_vector = lax.dynamic_slice_in_dim(vectors, (col_index * C).astype(jnp.int32), C, 1)
            forward, backward = tile_terms(row_vector, column_vector, near_blocks[row_index, col_index],
                                           far_left[row_index, col_index], far_right[row_index, col_index],
                                           far_mask[row_index, col_index], ranks[row_index, col_index],
                                           near_rows[row_index, col_index], near_cols[row_index, col_index])
            back_inner = back_inner.at[col_index].add(backward)
            return (fwd_total + forward, back_inner), None

        start_carry = (jnp.zeros((NRHS, S), jnp.float32), back_total)
        (fwd_total, back_total), unused = lax.scan(col_step, start_carry, jnp.arange(GRID_C, dtype=jnp.int32))
        return back_total, fwd_total

    back_total, fwd_rows = lax.scan(row_step, jnp.zeros((GRID_C, NRHS, C), jnp.float32), jnp.arange(GRID_R, dtype=jnp.int32))
    forward = jnp.transpose(fwd_rows, (1, 0, 2)).reshape(NRHS, ORDER)
    backward = jnp.transpose(back_total, (1, 0, 2)).reshape(NRHS, ORDER)
    return forward + backward
```

```python
import functools

import jax
import jax.numpy as jnp
from jax import lax
from jax.experimental import pallas as pl
from jax.experimental.pallas import tpu as pltpu
from jax.sharding import PartitionSpec as P

BF16 = jnp.bfloat16
F32 = jnp.float32
NT = (((1,), (1,)), ((), ()))


def spread(pieces, pieces_ref, flat_ref, width):
    block = flat_ref.shape[-1]
    for index, key in enumerate(pieces):
        start = index * width
        done = 0
        while done < width:
            at, offset = divmod(start + done, block)
            part = min(width - done, block - offset)
            flat_ref[at, :, offset : offset + part] = pieces_ref[key][:, done : done + part]
            done += part


def collect(total_ref, out_ref):
    block = total_ref.shape[-1]
    count, _, width = out_ref.shape
    for index in range(count):
        start = index * width
        done = 0
        while done < width:
            at, offset = divmod(start + done, block)
            part = min(width - done, block - offset)
            out_ref[index, :, done : done + part] = total_ref[
                at, :, offset : offset + part
            ].astype(out_ref.dtype)
            done += part


def half_kernel(
    in_keys,
    forward,
    mask_ref,
    rank_ref,
    in_at_ref,
    out_at_ref,
    x_ref,
    blocks_ref,
    in_factor_ref,
    out_factor_ref,
    out_ref,
    flat_ref,
    total_ref,
):
    width = out_ref.shape[-1]
    vectors = out_ref.shape[1]
    rank = in_factor_ref.shape[0]

    @pl.when(mask_ref[0] > 0)
    def far():
        coef = jnp.zeros((vectors, rank), F32)
        for index, key in enumerate(in_keys):
            coef += lax.dot_general(
                x_ref[key],
                in_factor_ref[:, index * width : (index + 1) * width],
                NT,
                preferred_element_type=F32,
            )
        keep = lax.broadcasted_iota(jnp.int32, (vectors, rank), 1) < rank_ref[0]
        coef = (coef * keep.astype(F32)).astype(BF16)
        for index in range(out_ref.shape[0]):
            out_ref[index] = jnp.dot(
                coef,
                out_factor_ref[:, index * width : (index + 1) * width],
                preferred_element_type=F32,
            ).astype(out_ref.dtype)

    @pl.when(mask_ref[0] <= 0)
    def near():
        spread(in_keys, x_ref, flat_ref, width)
        total_ref[...] = jnp.zeros_like(total_ref)
        for slot in range(blocks_ref.shape[0]):
            piece = flat_ref[in_at_ref[slot]]
            block = blocks_ref[slot]
            if forward:
                add = lax.dot_general(piece, block, NT, preferred_element_type=F32)
            else:
                add = jnp.dot(piece, block, preferred_element_type=F32)
            at = out_at_ref[slot]
            total_ref[at] = total_ref[at] + add
        collect(total_ref, out_ref)


def half(forward, in_keys, x, blocks, in_factor, out_factor, mask, rank, in_at, out_at):
    width = x.shape[-1]
    vectors = x.shape[-2]
    block = blocks.shape[-1]
    out_count = out_factor.shape[1] // width
    smem = pl.BlockSpec(memory_space=pltpu.SMEM)
    vmem = pl.BlockSpec(memory_space=pltpu.VMEM)
    return pl.pallas_call(
        functools.partial(half_kernel, in_keys, forward),
        out_shape=jax.ShapeDtypeStruct((out_count, vectors, width), BF16),
        in_specs=[smem] * 4 + [vmem] * 4,
        out_specs=vmem,
        scratch_shapes=[
            pltpu.VMEM((in_factor.shape[1] // block, vectors, block), BF16),
            pltpu.VMEM((out_factor.shape[1] // block, vectors, block), F32),
        ],
        compiler_params=pltpu.CompilerParams(vmem_limit_bytes=40 * 1024 * 1024),
        cost_estimate=pl.CostEstimate(
            flops=2 * vectors * blocks.size, bytes_accessed=2 * blocks.size, transcendentals=0
        ),
        name="forward_terms" if forward else "backward_terms",
    )(mask, rank, in_at, out_at, x, blocks, in_factor, out_factor)


def shards(
    rows, cols, vectors, near_blocks, far_left, far_right, far_mask, ranks, near_rows, near_cols
):
    half_cols = cols // 2
    take = [
        ((c // 2) * cols + (c % 2) * half_cols + r, r * cols + c)
        for r in range(rows)
        for c in range(cols)
    ]
    give = [(b, a) for a, b in take]
    blocks, left, right = near_blocks[0, 0], far_left[0, 0], far_right[0, 0]
    mask, rank = far_mask[0], ranks[0]
    rows_at, cols_at = near_rows[0, 0], near_cols[0, 0]

    piece = lax.ppermute(vectors, ("row", "col"), take)
    column_vector = lax.all_gather(piece, "row")
    forward = half(
        True,
        tuple((k,) for k in range(rows)),
        column_vector,
        blocks,
        right,
        left,
        mask,
        rank,
        cols_at,
        rows_at,
    )
    fwd_parts = lax.all_to_all(forward, "col", 0, 0)

    pairs = [[i, i + half_cols] for i in range(half_cols)]
    rings = [list(range(half_cols)), list(range(half_cols, cols))]
    both = lax.all_gather(vectors, "col", axis_index_groups=pairs)
    row_vector = lax.all_gather(both, "col", axis_index_groups=rings)
    backward = half(
        False,
        tuple((k % half_cols, k // half_cols) for k in range(cols)),
        row_vector,
        blocks,
        left,
        right,
        mask,
        rank,
        rows_at,
        cols_at,
    )
    back_parts = lax.all_to_all(backward, "row", 0, 0)
    back_sum = jnp.sum(back_parts.astype(F32), axis=0)
    mirrored = lax.ppermute(back_sum, ("row", "col"), give)
    fwd_sum = jnp.sum(fwd_parts.astype(F32), axis=0)
    return fwd_sum + mirrored


def solution(mesh):
    return jax.shard_map(
        functools.partial(shards, mesh.shape["row"], mesh.shape["col"]),
        mesh=mesh,
        in_specs=(
            P(None, ("row", "col")),
            P("row", "col", None, None, None),
            P("row", "col", None, None),
            P("row", "col", None, None),
            P("row", "col"),
            P("row", "col"),
            P("row", "col", None),
            P("row", "col", None),
        ),
        out_specs=P(None, ("row", "col")),
        check_vma=False,
    )
```

```python
import functools

import jax
import jax.numpy as jnp
from jax import lax
from jax.experimental import pallas as pl
from jax.experimental.pallas import tpu as pltpu
from jax.sharding import PartitionSpec as P

BF16 = jnp.bfloat16
F32 = jnp.float32
NT = (((1,), (1,)), ((), ()))
SMEM = pl.BlockSpec(memory_space=pltpu.SMEM)
VMEM = pl.BlockSpec(memory_space=pltpu.VMEM)
ANY = pl.BlockSpec(memory_space=pl.ANY)
PARAMS = pltpu.CompilerParams(vmem_limit_bytes=40 * 1024 * 1024)


def lanes(start, size):
    return pl.ds(pl.multiple_of(start, 128), size)


def coefficients(flat_ref, factor_ref, rank_ref):
    rank, span = factor_ref.shape
    step = 2048
    coef = jnp.zeros((flat_ref.shape[0], rank), F32)
    for start in range(0, span, step):
        coef += lax.dot_general(
            flat_ref[:, start : start + step],
            factor_ref[:, start : start + step],
            NT,
            preferred_element_type=F32,
        )
    keep = lax.broadcasted_iota(jnp.int32, coef.shape, 1) < rank_ref[0]
    return (coef * keep.astype(F32)).astype(BF16)


def forward_kernel(
    place_ref,
    mask_ref,
    rank_ref,
    rows_ref,
    cols_ref,
    x_ref,
    blocks_ref,
    left_ref,
    right_ref,
    kept_ref,
    sent_ref,
    flat_ref,
    total_ref,
):
    count, _, width = kept_ref.shape
    block = blocks_ref.shape[-1]
    own = place_ref[1] // count
    for index in range(x_ref.shape[0]):
        flat_ref[:, index * width : (index + 1) * width] = x_ref[index]

    @pl.when(mask_ref[0] > 0)
    def far():
        coef = coefficients(flat_ref, right_ref, rank_ref)
        for index in range(count):
            for half, out_ref in ((own, kept_ref), (1 - own, sent_ref)):
                at = lanes((half * count + index) * width, width)
                out_ref[index] = jnp.dot(
                    coef, left_ref[:, at], preferred_element_type=F32
                ).astype(out_ref.dtype)

    @pl.when(mask_ref[0] <= 0)
    def near():
        total_ref[...] = jnp.zeros_like(total_ref)
        for slot in range(blocks_ref.shape[0]):
            piece = flat_ref[:, lanes(cols_ref[slot] * block, block)]
            add = lax.dot_general(piece, blocks_ref[slot], NT, preferred_element_type=F32)
            at = lanes(rows_ref[slot] * block, block)
            total_ref[:, at] = total_ref[:, at] + add
        for index in range(count):
            for half, out_ref in ((own, kept_ref), (1 - own, sent_ref)):
                at = lanes((half * count + index) * width, width)
                out_ref[index] = total_ref[:, at].astype(out_ref.dtype)


def backward_kernel(
    shifts,
    place_ref,
    mask_ref,
    rank_ref,
    rows_ref,
    cols_ref,
    *refs,
):
    x_refs = refs[: len(shifts)]
    blocks_ref, left_ref, right_ref, kept_ref, sent_ref, flat_ref, total_ref = refs[len(shifts) :]
    count, _, width = kept_ref.shape
    ring = count * 2
    block = blocks_ref.shape[-1]
    own = place_ref[1] // ring
    z = place_ref[1] % ring
    core = place_ref[0] % 2
    for (shift, first), x_ref in zip(shifts, x_refs):
        for side in range(x_ref.shape[0]):
            half = own if side + first == 0 else 1 - own
            for far_step in range(x_ref.shape[1]):
                source = (z + ring - shift) % 4 + 4 * far_step
                at = lanes((half * ring + source) * width, width)
                flat_ref[:, at] = x_ref[side, far_step]

    @pl.when(mask_ref[0] > 0)
    def far():
        coef = coefficients(flat_ref, left_ref, rank_ref)
        for index in range(count):
            for bit, out_ref in ((core, kept_ref), (1 - core, sent_ref)):
                at = lanes((2 * index + bit) * width, width)
                out_ref[index] = jnp.dot(coef, right_ref[:, at], preferred_element_type=F32)

    @pl.when(mask_ref[0] <= 0)
    def near():
        total_ref[...] = jnp.zeros_like(total_ref)
        for slot in range(blocks_ref.shape[0]):
            piece = flat_ref[:, lanes(rows_ref[slot] * block, block)]
            add = jnp.dot(piece, blocks_ref[slot], preferred_element_type=F32)
            at = lanes(cols_ref[slot] * block, block)
            total_ref[:, at] = total_ref[:, at] + add
        for index in range(count):
            for bit, out_ref in ((core, kept_ref), (1 - core, sent_ref)):
                out_ref[index] = total_ref[:, lanes((2 * index + bit) * width, width)]


def copies_kernel(x_ref, out_ref):
    for index in range(out_ref.shape[0]):
        out_ref[index] = x_ref[...]


def pair_sum_kernel(a_ref, b_ref, out_ref):
    out_ref[...] = (a_ref[...] + b_ref[...].astype(F32)).astype(out_ref.dtype)


def split_sum_kernel(place_ref, a_ref, b_ref, kept_ref, sent_ref):
    bit = place_ref[0] // 2 % 2
    for index in range(kept_ref.shape[0]):
        for at, out_ref in ((2 * index + bit, kept_ref), (2 * index + 1 - bit, sent_ref)):
            out_ref[index] = a_ref[at] + b_ref[at]


def fan_sum_kernel(place_ref, a_ref, b_ref, *out_refs):
    y = place_ref[0] // 4
    for step, out_ref in enumerate(out_refs):
        at = (y + step) % len(out_refs)
        out_ref[...] = (a_ref[at] + b_ref[at]).astype(out_ref.dtype)


def after(count, kernel, *refs):
    kernel(*refs[count:])


def call(kernel, outs, ins, scalars=(), scratch=(), flops=0, name=None, waits=()):
    nbytes = sum(a.size * a.dtype.itemsize for a in (*ins, *outs))
    return pl.pallas_call(
        functools.partial(after, len(waits), kernel),
        out_shape=outs,
        in_specs=[ANY] * len(waits) + [SMEM] * len(scalars) + [VMEM] * len(ins),
        out_specs=[VMEM] * len(outs),
        scratch_shapes=scratch,
        compiler_params=PARAMS,
        cost_estimate=pl.CostEstimate(flops=flops, bytes_accessed=nbytes, transcendentals=0),
        name=name,
    )(*waits, *scalars, *ins)


def shards(
    rows, cols, vectors, near_blocks, far_left, far_right, far_mask, ranks, near_rows, near_cols
):
    ring = cols // 2
    vec, width = vectors.shape
    shape = jax.ShapeDtypeStruct
    blocks, left, right = near_blocks[0, 0], far_left[0, 0], far_right[0, 0]
    place = jnp.stack([lax.axis_index("row"), lax.axis_index("col")]).astype(jnp.int32)
    scalars = (place, far_mask[0], ranks[0], near_rows[0, 0], near_cols[0, 0])
    flops = 2 * vec * blocks.size

    def owner(r, c):
        return (c // 2) * cols + (c % 2) * ring + r

    def along_z(value, shift):
        pairs = [(i, i // ring * ring + (i % ring + shift) % ring) for i in range(cols)]
        return lax.ppermute(value, "col", pairs)

    def across_x(value):
        return lax.ppermute(value, "col", [(i, (i + ring) % cols) for i in range(cols)])

    def swap_row(value, bit):
        return lax.ppermute(value, "row", [(i, i ^ bit) for i in range(rows)])

    take = [(owner(r, c), r * cols + c) for r in range(rows) for c in range(cols)]
    piece = lax.ppermute(vectors, ("row", "col"), take)
    (copies,) = call(copies_kernel, [shape((rows, vec, width), BF16)], [piece], name="copies")
    column_vector = lax.all_to_all(copies, "row", 0, 0)

    fours = [[h + k for k in range(0, ring, 4)] for s in (0, ring) for h in range(s, s + 4)]
    quarter = lax.all_gather(vectors, "col", axis_index_groups=fours)
    both = jnp.stack([quarter, across_x(quarter)])
    shifts = ((0, 0), (1, 0), (-1, 0), (2, 0), (-2, 1))
    gathered = [
        both,
        along_z(both, 1),
        along_z(both, -1),
        along_z(both[:1], 2),
        along_z(both[1:], -2),
    ]

    kept, sent = call(
        forward_kernel,
        [shape((ring, vec, width), F32), shape((ring, vec, width), BF16)],
        [column_vector, blocks, left, right],
        scalars,
        [pltpu.VMEM((vec, right.shape[1]), BF16), pltpu.VMEM((vec, left.shape[1]), F32)],
        flops,
        "forward_terms",
        [both],
    )
    returned = across_x(sent)
    b_kept, b_sent = call(
        functools.partial(backward_kernel, shifts),
        [shape((rows // 2, vec, width), F32)] * 2,
        [*gathered, blocks, left, right],
        scalars,
        [pltpu.VMEM((vec, left.shape[1]), BF16), pltpu.VMEM((vec, right.shape[1]), F32)],
        flops,
        "backward_terms",
    )
    (halves,) = call(
        pair_sum_kernel,
        [shape((ring, vec, width), BF16)],
        [kept, returned],
        name="half_row",
        waits=[b_kept],
    )
    rings = [list(range(ring)), list(range(ring, cols))]
    fwd_parts = lax.all_to_all(halves, "col", 0, 0, axis_index_groups=rings)

    b_kept, b_sent = call(
        split_sum_kernel,
        [shape((rows // 4, vec, width), F32)] * 2,
        [b_kept, swap_row(b_sent, 1)],
        (place,),
        name="core_sum",
    )
    fans = call(
        fan_sum_kernel,
        [shape((vec, width), BF16)] * 4,
        [b_kept, swap_row(b_sent, 2)],
        (place,),
        name="pair_sum",
    )
    total = jnp.sum(fwd_parts.astype(F32), axis=0)
    for step, fan in enumerate(fans):
        pairs = [
            (r * cols + c, owner((r // 4 + step) % 4 * 4 + r % 4, c))
            for r in range(rows)
            for c in range(cols)
        ]
        total = total + lax.ppermute(fan, ("row", "col"), pairs).astype(F32)
    return total


def solution(mesh):
    return jax.shard_map(
        functools.partial(shards, mesh.shape["row"], mesh.shape["col"]),
        mesh=mesh,
        in_specs=(
            P(None, ("row", "col")),
            P("row", "col", None, None, None),
            P("row", "col", None, None),
            P("row", "col", None, None),
            P("row", "col"),
            P("row", "col"),
            P("row", "col", None),
            P("row", "col", None),
        ),
        out_specs=P(None, ("row", "col")),
        check_vma=False,
    )
```

```python
import functools

import jax
import jax.numpy as jnp
from jax import lax
from jax.experimental import pallas as pl
from jax.experimental.pallas import tpu as pltpu
from jax.sharding import PartitionSpec as P

BF16 = jnp.bfloat16
F32 = jnp.float32
NT = (((1,), (1,)), ((), ()))
SMEM = pl.BlockSpec(memory_space=pltpu.SMEM)
VMEM = pl.BlockSpec(memory_space=pltpu.VMEM)
ANY = pl.BlockSpec(memory_space=pl.ANY)
PARAMS = pltpu.CompilerParams(vmem_limit_bytes=40 * 1024 * 1024)


def lanes(start, size):
    return pl.ds(pl.multiple_of(start, 128), size)


def coefficients(flat_ref, factor_ref, rank_ref):
    rank, span = factor_ref.shape
    step = 2048
    coef = jnp.zeros((flat_ref.shape[0], rank), F32)
    for start in range(0, span, step):
        coef += lax.dot_general(
            flat_ref[:, start : start + step],
            factor_ref[:, start : start + step],
            NT,
            preferred_element_type=F32,
        )
    keep = lax.broadcasted_iota(jnp.int32, coef.shape, 1) < rank_ref[0]
    return (coef * keep.astype(F32)).astype(BF16)


def forward_kernel(
    place_ref,
    mask_ref,
    rank_ref,
    rows_ref,
    cols_ref,
    x_ref,
    blocks_ref,
    left_ref,
    right_ref,
    kept_ref,
    sent_ref,
    flat_ref,
    total_ref,
):
    count, _, width = kept_ref.shape
    block = blocks_ref.shape[-1]
    own = place_ref[1] // count
    for index in range(x_ref.shape[0]):
        flat_ref[:, index * width : (index + 1) * width] = x_ref[index]

    @pl.when(mask_ref[0] > 0)
    def far():
        coef = coefficients(flat_ref, right_ref, rank_ref)
        for index in range(count):
            for half, out_ref in ((own, kept_ref), (1 - own, sent_ref)):
                at = lanes((half * count + index) * width, width)
                out_ref[index] = jnp.dot(
                    coef, left_ref[:, at], preferred_element_type=F32
                ).astype(out_ref.dtype)

    @pl.when(mask_ref[0] <= 0)
    def near():
        total_ref[...] = jnp.zeros_like(total_ref)
        for slot in range(blocks_ref.shape[0]):
            piece = flat_ref[:, lanes(cols_ref[slot] * block, block)]
            add = lax.dot_general(piece, blocks_ref[slot], NT, preferred_element_type=F32)
            at = lanes(rows_ref[slot] * block, block)
            total_ref[:, at] = total_ref[:, at] + add
        for index in range(count):
            for half, out_ref in ((own, kept_ref), (1 - own, sent_ref)):
                at = lanes((half * count + index) * width, width)
                out_ref[index] = total_ref[:, at].astype(out_ref.dtype)


def backward_kernel(
    shifts,
    place_ref,
    mask_ref,
    rank_ref,
    rows_ref,
    cols_ref,
    *refs,
):
    x_refs = refs[: len(shifts)]
    blocks_ref, left_ref, right_ref, kept_ref, sent_ref, flat_ref, total_ref = refs[len(shifts) :]
    count, _, width = kept_ref.shape
    ring = count * 2
    block = blocks_ref.shape[-1]
    own = place_ref[1] // ring
    z = place_ref[1] % ring
    core = place_ref[0] % 2
    for (shift, first), x_ref in zip(shifts, x_refs):
        for step in range(x_ref.shape[0]):
            source = (z + ring - shift) % 4 + 4 * (first + step)
            for side, half in enumerate((own, 1 - own)):
                at = lanes((half * ring + source) * width, width)
                flat_ref[:, at] = x_ref[step, side]

    @pl.when(mask_ref[0] > 0)
    def far():
        coef = coefficients(flat_ref, left_ref, rank_ref)
        for index in range(count):
            for bit, out_ref in ((core, kept_ref), (1 - core, sent_ref)):
                at = lanes((2 * index + bit) * width, width)
                out_ref[index] = jnp.dot(coef, right_ref[:, at], preferred_element_type=F32)

    @pl.when(mask_ref[0] <= 0)
    def near():
        total_ref[...] = jnp.zeros_like(total_ref)
        for slot in range(blocks_ref.shape[0]):
            piece = flat_ref[:, lanes(rows_ref[slot] * block, block)]
            add = jnp.dot(piece, blocks_ref[slot], preferred_element_type=F32)
            at = lanes(cols_ref[slot] * block, block)
            total_ref[:, at] = total_ref[:, at] + add
        for index in range(count):
            for bit, out_ref in ((core, kept_ref), (1 - core, sent_ref)):
                out_ref[index] = total_ref[:, lanes((2 * index + bit) * width, width)]


def copies_kernel(x_ref, out_ref):
    for index in range(out_ref.shape[0]):
        out_ref[index] = x_ref[...]


def pair_sum_kernel(a_ref, b_ref, out_ref):
    out_ref[...] = (a_ref[...] + b_ref[...].astype(F32)).astype(out_ref.dtype)


def split_sum_kernel(place_ref, a_ref, b_ref, kept_ref, sent_ref):
    bit = place_ref[0] // 2 % 2
    for index in range(kept_ref.shape[0]):
        for at, out_ref in ((2 * index + bit, kept_ref), (2 * index + 1 - bit, sent_ref)):
            out_ref[index] = a_ref[at] + b_ref[at]


def fan_sum_kernel(place_ref, a_ref, b_ref, *out_refs):
    y = place_ref[0] // 4
    for step, out_ref in zip((1, 2, 3, 0), out_refs):
        at = (y + step) % len(out_refs)
        out_ref[...] = (a_ref[at] + b_ref[at]).astype(out_ref.dtype)


def add_kernel(own_ref, *refs):
    total = own_ref[...]
    for ref in refs[:-1]:
        total += ref[...].astype(F32)
    refs[-1][...] = total.astype(refs[-1].dtype)


def after(count, kernel, *refs):
    kernel(*refs[count:])


def call(kernel, outs, ins, scalars=(), scratch=(), flops=0, name=None, waits=()):
    nbytes = sum(a.size * a.dtype.itemsize for a in (*ins, *outs))
    return pl.pallas_call(
        functools.partial(after, len(waits), kernel),
        out_shape=outs,
        in_specs=[ANY] * len(waits) + [SMEM] * len(scalars) + [VMEM] * len(ins),
        out_specs=[VMEM] * len(outs),
        scratch_shapes=scratch,
        compiler_params=PARAMS,
        cost_estimate=pl.CostEstimate(flops=flops, bytes_accessed=nbytes, transcendentals=0),
        name=name,
    )(*waits, *scalars, *ins)


def shards(
    rows, cols, vectors, near_blocks, far_left, far_right, far_mask, ranks, near_rows, near_cols
):
    ring = cols // 2
    vec, width = vectors.shape
    shape = jax.ShapeDtypeStruct
    blocks, left, right = near_blocks[0, 0], far_left[0, 0], far_right[0, 0]
    place = jnp.stack([lax.axis_index("row"), lax.axis_index("col")]).astype(jnp.int32)
    scalars = (place, far_mask[0], ranks[0], near_rows[0, 0], near_cols[0, 0])
    flops = 2 * vec * blocks.size

    def owner(r, c):
        return (c // 2) * cols + (c % 2) * ring + r

    def along_z(value, shift):
        pairs = [(i, i // ring * ring + (i % ring + shift) % ring) for i in range(cols)]
        return lax.ppermute(value, "col", pairs)

    def across_x(value):
        return lax.ppermute(value, "col", [(i, (i + ring) % cols) for i in range(cols)])

    def swap_row(value, bit):
        return lax.ppermute(value, "row", [(i, i ^ bit) for i in range(rows)])

    fours = [[h + k for k in range(0, ring, 4)] for s in (0, ring) for h in range(s, s + 4)]
    partner = across_x(vectors)
    pair = jnp.stack([vectors, partner])
    quarter = lax.all_gather(pair, "col", axis_index_groups=fours)
    shifts = ((0, 0), (1, 0), (-1, 0), (2, 0), (-2, 2))
    gathered = [
        quarter,
        along_z(quarter, 1),
        along_z(quarter, -1),
        along_z(quarter[:2], 2),
        along_z(quarter[2:], -2),
    ]

    take = [(owner(r, c), r * cols + c) for r in range(rows) for c in range(cols)]
    piece = lax.ppermute(vectors, ("row", "col"), take)
    (copies,) = call(copies_kernel, [shape((rows, vec, width), BF16)], [piece], name="copies", waits=[partner])
    column_vector = lax.all_to_all(copies, "row", 0, 0)

    kept, sent = call(
        forward_kernel,
        [shape((ring, vec, width), F32), shape((ring, vec, width), BF16)],
        [column_vector, blocks, left, right],
        scalars,
        [pltpu.VMEM((vec, right.shape[1]), BF16), pltpu.VMEM((vec, left.shape[1]), F32)],
        flops,
        "forward_terms",
        [quarter],
    )
    returned = across_x(sent)
    b_kept, b_sent = call(
        functools.partial(backward_kernel, shifts),
        [shape((rows // 2, vec, width), F32)] * 2,
        [*gathered, blocks, left, right],
        scalars,
        [pltpu.VMEM((vec, left.shape[1]), BF16), pltpu.VMEM((vec, right.shape[1]), F32)],
        flops,
        "backward_terms",
        [returned],
    )
    b_kept, b_sent = call(
        split_sum_kernel,
        [shape((rows // 4, vec, width), F32)] * 2,
        [b_kept, swap_row(b_sent, 1)],
        (place,),
        name="core_sum",
    )
    (halves,) = call(
        pair_sum_kernel,
        [shape((ring, vec, width), BF16)],
        [kept, returned],
        name="half_row",
        waits=[b_kept],
    )
    rings = [list(range(ring)), list(range(ring, cols))]
    fwd_parts = lax.all_to_all(halves, "col", 0, 0, axis_index_groups=rings)

    y_parts = call(
        fan_sum_kernel,
        [shape((vec, width), F32)] * 4,
        [b_kept, swap_row(b_sent, 2)],
        (place,),
        name="pair_sum",
    )
    near = [
        lax.ppermute(part, "row", [(r, (r + 4 * step) % rows) for r in range(rows)])
        for step, part in zip((1, 2, 3), y_parts)
    ]
    (back_sum,) = call(add_kernel, [shape((vec, width), BF16)], [y_parts[3], *near], name="y_sum")
    mirrored = lax.ppermute(back_sum, ("row", "col"), [(b, a) for a, b in take])
    return jnp.sum(fwd_parts.astype(F32), axis=0) + mirrored.astype(F32)


def solution(mesh):
    return jax.shard_map(
        functools.partial(shards, mesh.shape["row"], mesh.shape["col"]),
        mesh=mesh,
        in_specs=(
            P(None, ("row", "col")),
            P("row", "col", None, None, None),
            P("row", "col", None, None),
            P("row", "col", None, None),
            P("row", "col"),
            P("row", "col"),
            P("row", "col", None),
            P("row", "col", None),
        ),
        out_specs=P(None, ("row", "col")),
        check_vma=False,
    )
```

```python
import functools

import jax
import jax.numpy as jnp
from jax import lax
from jax.experimental import pallas as pl
from jax.experimental.pallas import tpu as pltpu
from jax.sharding import PartitionSpec as P

BF16 = jnp.bfloat16
F32 = jnp.float32
NT = (((1,), (1,)), ((), ()))
SMEM = pl.BlockSpec(memory_space=pltpu.SMEM)
VMEM = pl.BlockSpec(memory_space=pltpu.VMEM)
ANY = pl.BlockSpec(memory_space=pl.ANY)
PARAMS = pltpu.CompilerParams(vmem_limit_bytes=40 * 1024 * 1024)


def lanes(start, size):
    return pl.ds(pl.multiple_of(start, 128), size)


def coefficients(flat_ref, factor_ref, rank_ref):
    rank, span = factor_ref.shape
    step = 2048
    coef = jnp.zeros((flat_ref.shape[0], rank), F32)
    for start in range(0, span, step):
        coef += lax.dot_general(
            flat_ref[:, start : start + step],
            factor_ref[:, start : start + step],
            NT,
            preferred_element_type=F32,
        )
    keep = lax.broadcasted_iota(jnp.int32, coef.shape, 1) < rank_ref[0]
    return (coef * keep.astype(F32)).astype(BF16)


def forward_kernel(
    place_ref,
    mask_ref,
    rank_ref,
    rows_ref,
    cols_ref,
    x_ref,
    blocks_hbm,
    left_hbm,
    right_hbm,
    kept_ref,
    sent_ref,
    flat_ref,
    total_ref,
    blocks_ref,
    left_ref,
    right_ref,
    sems,
):
    count, _, width = kept_ref.shape
    block = blocks_ref.shape[-1]
    own = place_ref[1] // count
    is_far = mask_ref[0] > 0
    blocks_copy = pltpu.make_async_copy(blocks_hbm, blocks_ref, sems.at[0])
    left_copy = pltpu.make_async_copy(left_hbm, left_ref, sems.at[1])
    right_copy = pltpu.make_async_copy(right_hbm, right_ref, sems.at[2])

    @pl.when(is_far)
    def fetch_factors():
        right_copy.start()
        left_copy.start()

    @pl.when(jnp.logical_not(is_far))
    def fetch_blocks():
        blocks_copy.start()

    for index in range(x_ref.shape[0]):
        flat_ref[:, index * width : (index + 1) * width] = x_ref[index]

    @pl.when(is_far)
    def far():
        right_copy.wait()
        left_copy.wait()
        coef = coefficients(flat_ref, right_ref, rank_ref)
        for index in range(count):
            for half, out_ref in ((own, kept_ref), (1 - own, sent_ref)):
                at = lanes((half * count + index) * width, width)
                out_ref[index] = jnp.dot(
                    coef, left_ref[:, at], preferred_element_type=F32
                ).astype(out_ref.dtype)

    @pl.when(jnp.logical_not(is_far))
    def near():
        total_ref[...] = jnp.zeros_like(total_ref)
        blocks_copy.wait()
        for slot in range(blocks_ref.shape[0]):
            piece = flat_ref[:, lanes(cols_ref[slot] * block, block)]
            add = lax.dot_general(piece, blocks_ref[slot], NT, preferred_element_type=F32)
            at = lanes(rows_ref[slot] * block, block)
            total_ref[:, at] = total_ref[:, at] + add
        for index in range(count):
            for half, out_ref in ((own, kept_ref), (1 - own, sent_ref)):
                at = lanes((half * count + index) * width, width)
                out_ref[index] = total_ref[:, at].astype(out_ref.dtype)


def backward_kernel(
    shifts,
    place_ref,
    mask_ref,
    rank_ref,
    rows_ref,
    cols_ref,
    *refs,
):
    x_refs = refs[: len(shifts)]
    blocks_ref, left_ref, right_ref, kept_ref, sent_ref, flat_ref, total_ref = refs[len(shifts) :]
    count, _, width = kept_ref.shape
    ring = count * 2
    block = blocks_ref.shape[-1]
    own = place_ref[1] // ring
    z = place_ref[1] % ring
    core = place_ref[0] % 2
    for (shift, first), x_ref in zip(shifts, x_refs):
        for step in range(x_ref.shape[0]):
            source = (z + ring - shift) % 4 + 4 * (first + step)
            for side, half in enumerate((own, 1 - own)):
                at = lanes((half * ring + source) * width, width)
                flat_ref[:, at] = x_ref[step, side]

    @pl.when(mask_ref[0] > 0)
    def far():
        coef = coefficients(flat_ref, left_ref, rank_ref)
        for index in range(count):
            for bit, out_ref in ((core, kept_ref), (1 - core, sent_ref)):
                at = lanes((2 * index + bit) * width, width)
                out_ref[index] = jnp.dot(coef, right_ref[:, at], preferred_element_type=F32)

    @pl.when(mask_ref[0] <= 0)
    def near():
        total_ref[...] = jnp.zeros_like(total_ref)
        for slot in range(blocks_ref.shape[0]):
            piece = flat_ref[:, lanes(rows_ref[slot] * block, block)]
            add = jnp.dot(piece, blocks_ref[slot], preferred_element_type=F32)
            at = lanes(cols_ref[slot] * block, block)
            total_ref[:, at] = total_ref[:, at] + add
        for index in range(count):
            for bit, out_ref in ((core, kept_ref), (1 - core, sent_ref)):
                out_ref[index] = total_ref[:, lanes((2 * index + bit) * width, width)]


def copies_kernel(x_ref, out_ref):
    for index in range(out_ref.shape[0]):
        out_ref[index] = x_ref[...]


def pair_sum_kernel(a_ref, b_ref, out_ref):
    out_ref[...] = (a_ref[...] + b_ref[...].astype(F32)).astype(out_ref.dtype)


def split_sum_kernel(place_ref, a_ref, b_ref, kept_ref, sent_ref):
    bit = place_ref[0] // 2 % 2
    for index in range(kept_ref.shape[0]):
        for at, out_ref in ((2 * index + bit, kept_ref), (2 * index + 1 - bit, sent_ref)):
            out_ref[index] = a_ref[at] + b_ref[at]


def fan_sum_kernel(place_ref, a_ref, b_ref, *out_refs):
    y = place_ref[0] // 4
    for step, out_ref in zip((1, 2, 3, 0), out_refs):
        at = (y + step) % len(out_refs)
        out_ref[...] = (a_ref[at] + b_ref[at]).astype(out_ref.dtype)


def add_kernel(own_ref, *refs):
    total = own_ref[...]
    for ref in refs[:-1]:
        total += ref[...].astype(F32)
    refs[-1][...] = total.astype(refs[-1].dtype)


def after(count, kernel, *refs):
    kernel(*refs[count:])


def call(
    kernel, outs, ins, scalars=(), scratch=(), flops=0, name=None, waits=(), fetched=()
):
    nbytes = sum(a.size * a.dtype.itemsize for a in (*ins, *fetched, *outs))
    return pl.pallas_call(
        functools.partial(after, len(waits), kernel),
        out_shape=outs,
        in_specs=[ANY] * len(waits) + [SMEM] * len(scalars) + [VMEM] * len(ins) + [ANY] * len(fetched),
        out_specs=[VMEM] * len(outs),
        scratch_shapes=scratch,
        compiler_params=PARAMS,
        cost_estimate=pl.CostEstimate(flops=flops, bytes_accessed=nbytes, transcendentals=0),
        name=name,
    )(*waits, *scalars, *ins, *fetched)


def shards(
    rows, cols, vectors, near_blocks, far_left, far_right, far_mask, ranks, near_rows, near_cols
):
    ring = cols // 2
    vec, width = vectors.shape
    shape = jax.ShapeDtypeStruct
    blocks, left, right = near_blocks[0, 0], far_left[0, 0], far_right[0, 0]
    place = jnp.stack([lax.axis_index("row"), lax.axis_index("col")]).astype(jnp.int32)
    scalars = (place, far_mask[0], ranks[0], near_rows[0, 0], near_cols[0, 0])
    flops = 2 * vec * blocks.size

    def owner(r, c):
        return (c // 2) * cols + (c % 2) * ring + r

    def along_z(value, shift):
        pairs = [(i, i // ring * ring + (i % ring + shift) % ring) for i in range(cols)]
        return lax.ppermute(value, "col", pairs)

    def across_x(value):
        return lax.ppermute(value, "col", [(i, (i + ring) % cols) for i in range(cols)])

    def swap_row(value, bit):
        return lax.ppermute(value, "row", [(i, i ^ bit) for i in range(rows)])

    fours = [[h + k for k in range(0, ring, 4)] for s in (0, ring) for h in range(s, s + 4)]
    partner = across_x(vectors)
    pair = jnp.stack([vectors, partner])
    quarter = lax.all_gather(pair, "col", axis_index_groups=fours)
    shifts = ((0, 0), (1, 0), (-1, 0), (2, 0), (-2, 2))
    gathered = [
        quarter,
        along_z(quarter, 1),
        along_z(quarter, -1),
        along_z(quarter[:2], 2),
        along_z(quarter[2:], -2),
    ]

    take = [(owner(r, c), r * cols + c) for r in range(rows) for c in range(cols)]
    piece = lax.ppermute(vectors, ("row", "col"), take)
    (copies,) = call(copies_kernel, [shape((rows, vec, width), BF16)], [piece], name="copies", waits=[partner])
    column_vector = lax.all_to_all(copies, "row", 0, 0)

    kept, sent = call(
        forward_kernel,
        [shape((ring, vec, width), F32), shape((ring, vec, width), BF16)],
        [column_vector],
        scalars,
        [pltpu.VMEM((vec, right.shape[1]), BF16), pltpu.VMEM((vec, left.shape[1]), F32)]
        + [pltpu.VMEM(a.shape, a.dtype) for a in (blocks, left, right)]
        + [pltpu.SemaphoreType.DMA((3,))],
        flops,
        "forward_terms",
        [quarter],
        [blocks, left, right],
    )
    returned = across_x(sent)
    b_kept, b_sent = call(
        functools.partial(backward_kernel, shifts),
        [shape((rows // 2, vec, width), F32)] * 2,
        [*gathered, blocks, left, right],
        scalars,
        [pltpu.VMEM((vec, left.shape[1]), BF16), pltpu.VMEM((vec, right.shape[1]), F32)],
        flops,
        "backward_terms",
        [returned],
    )
    b_kept, b_sent = call(
        split_sum_kernel,
        [shape((rows // 4, vec, width), F32)] * 2,
        [b_kept, swap_row(b_sent, 1)],
        (place,),
        name="core_sum",
    )
    (halves,) = call(
        pair_sum_kernel,
        [shape((ring, vec, width), BF16)],
        [kept, returned],
        name="half_row",
        waits=[b_kept],
    )
    rings = [list(range(ring)), list(range(ring, cols))]
    fwd_parts = lax.all_to_all(halves, "col", 0, 0, axis_index_groups=rings)

    y_parts = call(
        fan_sum_kernel,
        [shape((vec, width), F32)] * 4,
        [b_kept, swap_row(b_sent, 2)],
        (place,),
        name="pair_sum",
    )
    near = [
        lax.ppermute(part, "row", [(r, (r + 4 * step) % rows) for r in range(rows)])
        for step, part in zip((1, 2, 3), y_parts)
    ]
    (back_sum,) = call(add_kernel, [shape((vec, width), BF16)], [y_parts[3], *near], name="y_sum")
    mirrored = lax.ppermute(back_sum, ("row", "col"), [(b, a) for a, b in take])
    return jnp.sum(fwd_parts.astype(F32), axis=0) + mirrored.astype(F32)


def solution(mesh):
    return jax.shard_map(
        functools.partial(shards, mesh.shape["row"], mesh.shape["col"]),
        mesh=mesh,
        in_specs=(
            P(None, ("row", "col")),
            P("row", "col", None, None, None),
            P("row", "col", None, None),
            P("row", "col", None, None),
            P("row", "col"),
            P("row", "col"),
            P("row", "col", None),
            P("row", "col", None),
        ),
        out_specs=P(None, ("row", "col")),
        check_vma=False,
    )
```
